256 devices in a mesh: space: 32 (over z_lo, x, core), filt: 8 (over z_hi, y).
Axes of the slice: x: 4, y: 4, z: 8 (z_hi: 2, z_lo: 4; z = z_hi * 4 + z_lo), core: 2. Of those that a mesh axis runs over, the one named last changes fastest.
Arguments:
- activations: bfloat16 [64, 32, 56, 128], P('filt', 'space'), may hold values from -6 to 6
- kernel: bfloat16 [64, 64, 3, 3, 3], P('filt'), may hold values from -0.15625 to 0.15625
- preact: bfloat16 [64, 32, 56, 128], P('filt', 'space'), may hold values from -6 to 6
- upstream: bfloat16 [64, 32, 56, 128], P('filt', 'space'), may hold values from -6 to 6
Outputs:
- input_grad: bfloat16 [64, 32, 56, 128], P('filt', 'space')
- kernel_grad: float32 [64, 64, 3, 3, 3], P('filt')
The draws below stay inside these ranges and needn't reach their ends.
All inputs are finite; a program needn't handle non-finite values.
Results may differ from the reference program's by a relative error of at most 0.0015.
Values may be sent and summed in bfloat16 or wider, within the bound.
No kernel may reach another device: no remote copies, remote signals or barrier semaphores. Data moves between devices by JAX's collectives and lax.ppermute only.
A program may use at most 128 MiB of HBM per device.

```python
import jax
import jax.numpy as jnp

CIN = 64
COUT = 64
H = 56
W = 128
NZ = 32


def level_of(key, shape, cuts, low, top_value):
    factor_of = 1.0
    for position, shards_of in cuts:
        draws = jax.random.uniform(jax.random.fold_in(jax.random.fold_in(key, 6), position), (shards_of,), jnp.float32, low / len(cuts), top_value / len(cuts))
        factor_of = factor_of * jnp.repeat(jnp.exp(draws), shape[position] // shards_of).reshape((-1,) + (1,) * (len(shape) - 1 - position))
    return factor_of


def scatter_about(own_key, dims, spread, reach, split=(), dtype=jnp.bfloat16):
    result = spread * jax.random.normal(own_key, dims, jnp.float32)
    if split:
        result = result * level_of(own_key, dims, split, -0.22, 0.18)
    return jnp.clip(result, -reach, reach).astype(dtype)


def setup_inputs(seed: int = 0) -> dict:
    key_list = jax.random.split(jax.random.key(seed), 5)
    return {
        "activations": scatter_about(key_list[0], (CIN, NZ, H, W), 1.0, 6.0, ((0, 8), (1, 32))),
        "kernel": scatter_about(key_list[1], (COUT, CIN, 3, 3, 3), (CIN * 27) ** -0.5, 0.15625, ((0, 8),)),
        "preact": scatter_about(key_list[2], (COUT, NZ, H, W), 1.0, 6.0, ((0, 8), (1, 32))),
        "upstream": scatter_about(key_list[3], (COUT, NZ, H, W), 1.0, 6.0, ((0, 8), (1, 32))),
    }


def data_grad(grad_pad, weight):
    chans = weight.shape[1]
    depth = grad_pad.shape[1] - 2
    rows = grad_pad.shape[2] - 2
    cols = grad_pad.shape[3] - 2
    total = jnp.zeros((chans, depth, rows, cols), jnp.float32)
    for depth_off in range(3):
        for row_off in range(3):
            for col_off in range(3):
                piece = grad_pad[:, 2 - depth_off:2 - depth_off + depth, 2 - row_off:2 - row_off + rows, 2 - col_off:2 - col_off + cols]
                total = total + jnp.einsum('fc,fzyx->czyx', weight[:, :, depth_off, row_off, col_off], piece)
    return total

def weight_grad(grad, input_pad):
    depth, rows, cols = (grad.shape[1], grad.shape[2], grad.shape[3])
    terms = []
    for depth_off in range(3):
        for row_off in range(3):
            for col_off in range(3):
                piece = input_pad[:, depth_off:depth_off + depth, row_off:row_off + rows, col_off:col_off + cols]
                terms.append(jnp.einsum('fzyx,czyx->fc', grad, piece))
    stacked = jnp.stack(terms, axis=-1)
    return stacked.reshape(grad.shape[0], input_pad.shape[0], 3, 3, 3)

def reference(activations, kernel, preact, upstream):
    masked = jnp.where(preact > 0, upstream, jnp.zeros_like(upstream))
    grad32 = masked.astype(jnp.float32)
    input32 = activations.astype(jnp.float32)
    weight32 = kernel.astype(jnp.float32)
    widths = ((0, 0), (1, 1), (1, 1), (1, 1))
    input_grad = data_grad(jnp.pad(grad32, widths), weight32).astype(jnp.bfloat16)
    scale = 1.0 / jnp.sqrt(jnp.float32(NZ * H * W))
    kernel_grad = weight_grad(grad32, jnp.pad(input32, widths)) * scale
    return (input_grad, kernel_grad)
```

```python
import jax
import jax.numpy as jnp
from jax import lax
from jax.experimental import pallas as pl
from jax.experimental.pallas import tpu as pltpu
from jax.sharding import PartitionSpec as P

ROWS, COLS, CH = 56, 128, 8
BF, F32 = jnp.bfloat16, jnp.float32


def space_pairs(to):
    pairs = []
    for i in range(32):
        z, x, core = to(i >> 3, (i >> 1) & 3, i & 1)
        pairs.append((i, ((z % 4) * 4 + x % 4) * 2 + core))
    return pairs


def filt_pairs(to):
    pairs = []
    for i in range(8):
        h, y = to(i >> 2, i & 3)
        pairs.append((i, h * 4 + y % 4))
    return pairs


UP = [(i, i + 1) for i in range(31)]
DOWN = [(i + 1, i) for i in range(31)]
CORE = space_pairs(lambda z, x, core: (z, x, core ^ 1))
X_OTHERS = [space_pairs(lambda z, x, core, j=j: (z, x + j, core)) for j in (1, 3, 2)]
Z_OTHERS = [space_pairs(lambda z, x, core, j=j: (z ^ j, x, core)) for j in (1, 2, 3)]
HALF = filt_pairs(lambda h, y: (h ^ 1, y))
Y_OTHERS = [filt_pairs(lambda h, y, j=j: (h, y + j)) for j in (1, 3, 2)]
Y_BACK = [filt_pairs(lambda h, y, j=j: (h, y - j)) for j in (1, 3, 2)]


def place():
    space, filt = lax.axis_index("space"), lax.axis_index("filt")
    return space % 2, filt // 4, filt % 4


def params():
    return pltpu.CompilerParams(vmem_limit_bytes=40 * 1024 * 1024)


def whole(count):
    return [pl.BlockSpec(memory_space=pltpu.VMEM)] * count


def mask_body(pre_ref, up_ref, kern_ref, out_ref):
    for f in range(CH):
        keep = pre_ref[f].astype(F32) > 0
        out_ref[f] = jnp.where(keep, up_ref[f].astype(F32), 0.0).astype(BF)
    blank = jnp.zeros((CH, 64), F32)
    for plane in range(2):
        pieces = []
        for k2 in range(7 * plane, 7 * plane + 7):
            even = kern_ref[2 * k2].astype(F32)
            odd = kern_ref[2 * k2 + 1].astype(F32) if 2 * k2 + 1 < 27 else blank
            pieces.append(jnp.concatenate([even, odd], axis=1))
        out_ref[CH + plane] = jnp.concatenate(pieces, axis=0).astype(BF)


def mask_call(preact, upstream, kern):
    return pl.pallas_call(
        mask_body,
        out_shape=jax.ShapeDtypeStruct((CH + 2, ROWS, COLS), BF),
        in_specs=whole(3),
        out_specs=pl.BlockSpec(memory_space=pltpu.VMEM),
        compiler_params=params(),
        cost_estimate=pl.CostEstimate(flops=100_000, bytes_accessed=500_000, transcendentals=0),
        name="mask",
    )(preact, upstream, kern)


def spread(ref, planes, scratch):
    for ch in range(planes):
        scratch[pl.ds(ch * ROWS, ROWS), :] = ref[ch].astype(F32)


def row_of(scratch, row):
    return scratch[pl.ds(row, CH, stride=ROWS), :]


def column_shifts(scratch, row, lane):
    block = row_of(scratch, row)
    left = jnp.where(lane == COLS - 1, 0.0, pltpu.roll(block, COLS - 1, 1))
    right = jnp.where(lane == 0, 0.0, pltpu.roll(block, 1, 1))
    return [left, block, right]


def shifted_rows(scratches, rows, lane):
    columns = []
    for row in rows:
        pieces = []
        for scratch in scratches:
            pieces += column_shifts(scratch, row, lane)
        columns.append(jnp.concatenate(pieces, axis=0).astype(BF))
    return jnp.concatenate(columns, axis=1)


def weight_body(m0, m1, m2, m3, *refs):
    acts, (keep_ref, send_ref), scratch = refs[:6], refs[6:8], refs[8:]
    core, _, _ = place()
    masked, planes = scratch[:4], scratch[4:]
    for ref, buf in zip((m0, m1, m2, m3), masked):
        spread(ref, CH, buf)
    for ref, buf in zip(acts, planes):
        spread(ref, CH, buf)
    lane = lax.broadcasted_iota(jnp.int32, (CH, COLS), 1)
    zero = jnp.zeros((CH, COLS), F32)
    gap = jnp.zeros((COLS - 9 * CH, COLS), F32)
    total = jnp.zeros((96, 256), F32)
    step = 8
    for first in range(0, ROWS, step):
        rows = range(first, first + step)
        lhs = shifted_rows(masked, rows, lane)
        columns = []
        for row in rows:
            pieces = []
            for block in range(2):
                for kz in range(3):
                    for ky in range(3):
                        at = row + ky - 1
                        inside = 0 <= at < ROWS
                        pieces.append(row_of(planes[3 * block + kz], at) if inside else zero)
                pieces.append(gap)
            columns.append(jnp.concatenate(pieces, axis=0).astype(BF))
        rhs = jnp.concatenate(columns, axis=1)
        total = total + lax.dot_general(
            lhs, rhs, (((1,), (1,)), ((), ())), preferred_element_type=F32
        )
    own, other = total[:, :COLS], total[:, COLS:]
    first_core = core == 0
    keep_ref[...] = jnp.where(first_core, own, other)
    send_ref[...] = jnp.where(first_core, other, own)


def weight_call(masked, acts):
    shape = jax.ShapeDtypeStruct((96, COLS), F32)
    return pl.pallas_call(
        weight_body,
        out_shape=(shape, shape),
        in_specs=whole(10),
        out_specs=tuple(whole(2)),
        scratch_shapes=[pltpu.VMEM((CH * ROWS, COLS), F32)] * 10,
        compiler_params=params(),
        cost_estimate=pl.CostEstimate(
            flops=2 * 96 * 256 * 7168, bytes_accessed=1_500_000, transcendentals=0
        ),
        name="weight_grad",
    )(*masked, *acts)


def data_body(m0, m1, m2, m3, down_ref, mid_ref, up_ref, *masked):
    _, half, y = place()
    for ref, buf in zip((m0, m1, m2, m3), masked):
        spread(ref, CH, buf)
    lane = lax.broadcasted_iota(jnp.int32, (CH, COLS), 1)
    rows = []
    for ref in (m0, m1, m2, m3):
        parts = [ref[CH].astype(F32), ref[CH + 1].astype(F32)]
        for kx in range(3):
            sums = [jnp.zeros((CH, COLS), F32) for _ in range(2)]
            for q in range(9):
                k = 3 * q + kx
                pair, odd = k // 2, k % 2
                value = parts[pair // 7][(pair % 7) * CH : (pair % 7 + 1) * CH]
                for block in range(2):
                    start = 8 * (4 * (half ^ block) + y)
                    shift = lax.rem(8 * q + 256 - 64 * odd - start, 128)
                    moved = pltpu.roll(value, shift, 1)
                    here = (lane >= 8 * q) & (lane < 8 * q + 8)
                    sums[block] = jnp.where(here, moved, sums[block])
            rows.append(jnp.concatenate(sums, axis=1))
    weights = jnp.concatenate(rows + [jnp.zeros((32, 256), F32)], axis=0)
    weights = jnp.transpose(weights)
    weights = jnp.concatenate([weights[:72, :96], weights[128:200, :96]], axis=0).astype(BF)
    outs = (down_ref, mid_ref, up_ref)
    sums = {}
    step = 4
    for first in range(0, ROWS, step):
        got = jnp.dot(
            weights, shifted_rows(masked, range(first, first + step), lane), preferred_element_type=F32
        )
        for i in range(step):
            row = first + i
            for block in range(2):
                for kz in range(3):
                    for ky in range(3):
                        at = row + ky - 1
                        if not 0 <= at < ROWS:
                            continue
                        top = ((block * 3 + kz) * 3 + ky) * CH
                        term = got[top : top + CH, i * COLS : (i + 1) * COLS]
                        key = (block, kz, at)
                        sums[key] = sums[key] + term if key in sums else term
                    done = [row - 1] if row < ROWS - 1 else [row - 1, row]
                    for at in done:
                        if at >= 0:
                            outs[kz][pl.ds(block * CH * ROWS + at, CH, stride=ROWS), :] = sums.pop(
                                (block, kz, at)
                            )


def data_call(masked):
    shape = jax.ShapeDtypeStruct((2 * CH * ROWS, COLS), F32)
    return pl.pallas_call(
        data_body,
        out_shape=(shape, shape, shape),
        in_specs=whole(4),
        out_specs=tuple(whole(3)),
        scratch_shapes=[pltpu.VMEM((CH * ROWS, COLS), F32)] * 4,
        compiler_params=params(),
        cost_estimate=pl.CostEstimate(
            flops=2 * 144 * 96 * 7168, bytes_accessed=2_000_000, transcendentals=0
        ),
        name="data_grad",
    )(*masked)


def final_body(scale, mine_ref, theirs_ref, out_ref):
    core, half, y = place()
    lane = lax.broadcasted_iota(jnp.int32, (24, COLS), 1)
    sources = []
    for ref, part in ((mine_ref, half ^ core), (theirs_ref, half ^ core ^ 1)):
        for j, away in enumerate((0, 1, 3, 2)):
            block = 4 * part + lax.rem(y + away, 4)
            sources.append((block, ref[24 * j : 24 * j + 24]))
    for q in range(9):
        total = jnp.zeros((24, COLS), F32)
        for block, value in sources:
            moved = pltpu.roll(value, lax.rem(8 * block + 128 - 8 * q, 128), 1)
            here = (lane >= 8 * block) & (lane < 8 * block + 8)
            total = jnp.where(here, moved, total)
        out_ref[24 * q : 24 * q + 24] = (total * scale)[:, :64]


def final_call(mine, theirs, scale):
    return pl.pallas_call(
        lambda *refs: final_body(scale, *refs),
        out_shape=jax.ShapeDtypeStruct((216, 64), F32),
        in_specs=whole(2),
        out_specs=pl.BlockSpec(memory_space=pltpu.VMEM),
        compiler_params=params(),
        cost_estimate=pl.CostEstimate(flops=100_000, bytes_accessed=200_000, transcendentals=0),
        name="place_blocks",
    )(mine, theirs)


def on_device(activations, kernel, preact, upstream):
    layers = lax.axis_size("space") * activations.shape[1]
    scale = (
        1.0 / float(layers * ROWS * COLS) ** 0.5
    )
    acts, pre, ups = (array[:, 0] for array in (activations, preact, upstream))
    kern = jnp.transpose(kernel, (2, 3, 4, 0, 1)).reshape(27, CH, 64)
    other = lax.ppermute(acts, "filt", HALF)
    mine = mask_call(pre, ups, kern)
    masked = [mine] + [lax.ppermute(mine, "filt", pairs) for pairs in Y_OTHERS]
    low, high = lax.ppermute(acts, "space", UP), lax.ppermute(acts, "space", DOWN)
    other_low, other_high = lax.ppermute(other, "space", UP), lax.ppermute(other, "space", DOWN)

    down, mid, up = data_call(masked)
    keep, send = weight_call(masked, (low, acts, high, other_low, other, other_high))

    terms = keep + lax.ppermute(send, "space", CORE)
    terms = sum([lax.ppermute(terms, "space", pairs) for pairs in X_OTHERS], terms)
    terms = sum([lax.ppermute(terms, "space", pairs) for pairs in Z_OTHERS], terms)
    blocks = [terms[24 * j : 24 * j + 24] for j in range(4)]
    got = [lax.ppermute(block, "filt", pairs) for block, pairs in zip(blocks[1:], Y_BACK)]
    mine_blocks = jnp.concatenate([blocks[0]] + got, axis=0)
    their_blocks = lax.ppermute(mine_blocks, "space", CORE)
    grads = final_call(mine_blocks, their_blocks, scale)
    kernel_grad = jnp.transpose(grads.reshape(3, 3, 3, CH, 64), (3, 4, 0, 1, 2))

    layer = mid + lax.ppermute(down, "space", DOWN) + lax.ppermute(up, "space", UP)
    own, away = layer[: CH * ROWS], layer[CH * ROWS :]
    own = own + lax.ppermute(away, "filt", HALF)
    input_grad = own.astype(BF).reshape(CH, 1, ROWS, COLS)
    return (input_grad, kernel_grad)


def solution(mesh):
    in_specs = (
        P("filt", "space", None, None),
        P("filt", None, None, None, None),
        P("filt", "space", None, None),
        P("filt", "space", None, None),
    )
    out_specs = (P("filt", "space", None, None), P("filt", None, None, None, None))
    return jax.shard_map(
        on_device, mesh=mesh, in_specs=in_specs, out_specs=out_specs, check_vma=False
    )
```

```python
import jax
import jax.numpy as jnp
from jax import lax
from jax.experimental import pallas as pl
from jax.experimental.pallas import tpu as pltpu
from jax.sharding import PartitionSpec as P

ROWS, COLS, CH = 56, 128, 8
BF, F32 = jnp.bfloat16, jnp.float32
COST = 20_000_000_000


def space_pairs(to):
    pairs = []
    for i in range(32):
        z, x, core = to(i >> 3, (i >> 1) & 3, i & 1)
        pairs.append((i, ((z % 4) * 4 + x % 4) * 2 + core))
    return pairs


def filt_pairs(to):
    pairs = []
    for i in range(8):
        h, y = to(i >> 2, i & 3)
        pairs.append((i, h * 4 + y % 4))
    return pairs


OUTER = [pair for i in range(1, 31, 2) for pair in ((i, i + 1), (i + 1, i))]
CORE = space_pairs(lambda z, x, core: (z, x, core ^ 1))
X_OTHERS = [space_pairs(lambda z, x, core, j=j: (z, x + j, core)) for j in (1, 3, 2)]
Z_OTHERS = [space_pairs(lambda z, x, core, j=j: (z ^ j, x, core)) for j in (1, 2, 3)]
HALF = filt_pairs(lambda h, y: (h ^ 1, y))
Y_OTHERS = [filt_pairs(lambda h, y, j=j: (h, y + j)) for j in (1, 3, 2)]
Y_BACK = [filt_pairs(lambda h, y, j=j: (h, y - j)) for j in (1, 3, 2)]


def place():
    space, filt = lax.axis_index("space"), lax.axis_index("filt")
    return space % 2, filt // 4, filt % 4


def params():
    return pltpu.CompilerParams(vmem_limit_bytes=40 * 1024 * 1024)


def whole(count):
    return [pl.BlockSpec(memory_space=pltpu.VMEM)] * count


def mask_body(pre_hbm, up_hbm, kern_hbm, out_ref, pre_ref, up_ref, kern_ref, sems):
    pairs = ((pre_hbm, pre_ref), (up_hbm, up_ref), (kern_hbm, kern_ref))
    copies = [pltpu.make_async_copy(src, dst, sems.at[i]) for i, (src, dst) in enumerate(pairs)]
    for copy in copies:
        copy.start()
    copies[0].wait()
    copies[1].wait()
    for f in range(CH):
        keep = pre_ref[f].astype(F32) > 0
        out_ref[f] = jnp.where(keep, up_ref[f].astype(F32), 0.0).astype(BF)
    copies[2].wait()
    blank = jnp.zeros((CH, 64), F32)
    for plane in range(2):
        pieces = []
        for k2 in range(7 * plane, 7 * plane + 7):
            even = kern_ref[2 * k2].astype(F32)
            odd = kern_ref[2 * k2 + 1].astype(F32) if 2 * k2 + 1 < 27 else blank
            pieces.append(jnp.concatenate([even, odd], axis=1))
        out_ref[CH + plane] = jnp.concatenate(pieces, axis=0).astype(BF)


def mask_call(preact, upstream, kern):
    return pl.pallas_call(
        mask_body,
        out_shape=jax.ShapeDtypeStruct((CH + 2, ROWS, COLS), BF),
        in_specs=[pl.BlockSpec(memory_space=pl.ANY)] * 3,
        out_specs=pl.BlockSpec(memory_space=pltpu.VMEM),
        scratch_shapes=[
            pltpu.VMEM((CH, ROWS, COLS), BF),
            pltpu.VMEM((CH, ROWS, COLS), BF),
            pltpu.VMEM((27, CH, 64), BF),
            pltpu.SemaphoreType.DMA((3,)),
        ],
        cost_estimate=pl.CostEstimate(flops=COST, bytes_accessed=500_000, transcendentals=0),
        name="mask",
    )(preact, upstream, kern)


def spread(ref, planes, scratch):
    for ch in range(planes):
        scratch[pl.ds(ch * ROWS, ROWS), :] = ref[ch].astype(F32)


def spread_either(first, ref, other, planes, scratch):
    for ch in range(planes):
        value = jnp.where(first, ref[ch].astype(F32), other[ch].astype(F32))
        scratch[pl.ds(ch * ROWS, ROWS), :] = value


def row_of(scratch, row):
    return scratch[pl.ds(row, CH, stride=ROWS), :]


def column_shifts(scratch, row, lane):
    block = row_of(scratch, row)
    left = jnp.where(lane == COLS - 1, 0.0, pltpu.roll(block, COLS - 1, 1))
    right = jnp.where(lane == 0, 0.0, pltpu.roll(block, 1, 1))
    return [left, block, right]


def shifted_rows(scratches, rows, lane):
    columns = []
    for row in rows:
        pieces = []
        for scratch in scratches:
            pieces += column_shifts(scratch, row, lane)
        columns.append(jnp.concatenate(pieces, axis=0).astype(BF))
    return jnp.concatenate(columns, axis=1)


def weight_body(m0, m1, m2, m3, *refs):
    acts, (keep_ref, send_ref), scratch = refs[:4], refs[4:6], refs[6:]
    core, _, _ = place()
    masked, planes = scratch[:4], scratch[4:]
    for ref, buf in zip((m0, m1, m2, m3), masked):
        spread(ref, CH, buf)
    first_core = core == 0
    inner, outer = acts[2:]
    for block in range(2):
        below, here, above = planes[3 * block : 3 * block + 3]
        near, far = (ref.at[pl.ds(CH * block, CH)] for ref in (inner, outer))
        spread_either(first_core, far, near, CH, below)
        spread(acts[block], CH, here)
        spread_either(first_core, near, far, CH, above)
    lane = lax.broadcasted_iota(jnp.int32, (CH, COLS), 1)
    zero = jnp.zeros((CH, COLS), F32)
    gap = jnp.zeros((COLS - 9 * CH, COLS), F32)
    total = jnp.zeros((96, 256), F32)
    step = 8
    for first in range(0, ROWS, step):
        rows = range(first, first + step)
        lhs = shifted_rows(masked, rows, lane)
        columns = []
        for row in rows:
            pieces = []
            for block in range(2):
                for kz in range(3):
                    for ky in range(3):
                        at = row + ky - 1
                        inside = 0 <= at < ROWS
                        pieces.append(row_of(planes[3 * block + kz], at) if inside else zero)
                pieces.append(gap)
            columns.append(jnp.concatenate(pieces, axis=0).astype(BF))
        rhs = jnp.concatenate(columns, axis=1)
        total = total + lax.dot_general(
            lhs, rhs, (((1,), (1,)), ((), ())), preferred_element_type=F32
        )
    own, other = total[:, :COLS], total[:, COLS:]
    keep_ref[...] = jnp.where(first_core, own, other)
    send_ref[...] = jnp.where(first_core, other, own)


def weight_call(masked, acts):
    shape = jax.ShapeDtypeStruct((96, COLS), F32)
    return pl.pallas_call(
        weight_body,
        out_shape=(shape, shape),
        in_specs=whole(8),
        out_specs=tuple(whole(2)),
        scratch_shapes=[pltpu.VMEM((CH * ROWS, COLS), F32)] * 10,
        compiler_params=params(),
        cost_estimate=pl.CostEstimate(
            flops=COST, bytes_accessed=1_500_000, transcendentals=0
        ),
        name="weight_grad",
    )(*masked, *acts)


def data_body(m0, m1, m2, m3, inner_ref, mid_ref, outer_ref, *masked):
    core, half, y = place()
    first_core = core == 0
    for ref, buf in zip((m0, m1, m2, m3), masked):
        spread(ref, CH, buf)
    lane = lax.broadcasted_iota(jnp.int32, (CH, COLS), 1)
    rows = []
    for ref in (m0, m1, m2, m3):
        parts = [ref[CH].astype(F32), ref[CH + 1].astype(F32)]
        for kx in range(3):
            sums = [jnp.zeros((CH, COLS), F32) for _ in range(2)]
            for q in range(9):
                k = 3 * q + kx
                pair, odd = k // 2, k % 2
                value = parts[pair // 7][(pair % 7) * CH : (pair % 7 + 1) * CH]
                for block in range(2):
                    start = 8 * (4 * (half ^ block) + y)
                    shift = lax.rem(8 * q + 256 - 64 * odd - start, 128)
                    moved = pltpu.roll(value, shift, 1)
                    here = (lane >= 8 * q) & (lane < 8 * q + 8)
                    sums[block] = jnp.where(here, moved, sums[block])
            rows.append(jnp.concatenate(sums, axis=1))
    weights = jnp.concatenate(rows + [jnp.zeros((32, 256), F32)], axis=0)
    weights = jnp.transpose(weights)
    weights = jnp.concatenate([weights[:72, :96], weights[128:200, :96]], axis=0).astype(BF)
    sums = {}
    step = 4
    for first in range(0, ROWS, step):
        got = jnp.dot(
            weights, shifted_rows(masked, range(first, first + step), lane), preferred_element_type=F32
        )
        for i in range(step):
            row = first + i
            for block in range(2):
                for kz in range(3):
                    for ky in range(3):
                        at = row + ky - 1
                        if not 0 <= at < ROWS:
                            continue
                        top = ((block * 3 + kz) * 3 + ky) * CH
                        term = got[top : top + CH, i * COLS : (i + 1) * COLS]
                        key = (block, kz, at)
                        sums[key] = sums[key] + term if key in sums else term
                done = [row - 1] if row < ROWS - 1 else [row - 1, row]
                for at in done:
                    if at >= 0:
                        down, mid, up = (sums.pop((block, kz, at)) for kz in range(3))
                        place_at = pl.ds(block * CH * ROWS + at, CH, stride=ROWS)
                        mid_ref[place_at, :] = mid
                        inner_ref[place_at, :] = jnp.where(first_core, up, down)
                        outer_ref[place_at, :] = jnp.where(first_core, down, up)


def data_call(masked):
    shape = jax.ShapeDtypeStruct((2 * CH * ROWS, COLS), F32)
    return pl.pallas_call(
        data_body,
        out_shape=(shape, shape, shape),
        in_specs=whole(4),
        out_specs=tuple(whole(3)),
        scratch_shapes=[pltpu.VMEM((CH * ROWS, COLS), F32)] * 4,
        compiler_params=params(),
        cost_estimate=pl.CostEstimate(
            flops=COST, bytes_accessed=2_000_000, transcendentals=0
        ),
        name="data_grad",
    )(*masked)


def final_body(scale, mine_ref, theirs_ref, out_ref):
    core, half, y = place()
    lane = lax.broadcasted_iota(jnp.int32, (24, COLS), 1)
    sources = []
    for ref, part in ((mine_ref, half ^ core), (theirs_ref, half ^ core ^ 1)):
        for j, away in enumerate((0, 1, 3, 2)):
            block = 4 * part + lax.rem(y + away, 4)
            sources.append((block, ref[24 * j : 24 * j + 24]))
    for q in range(9):
        total = jnp.zeros((24, COLS), F32)
        for block, value in sources:
            moved = pltpu.roll(value, lax.rem(8 * block + 128 - 8 * q, 128), 1)
            here = (lane >= 8 * block) & (lane < 8 * block + 8)
            total = jnp.where(here, moved, total)
        out_ref[24 * q : 24 * q + 24] = (total * scale)[:, :64]


def final_call(mine, theirs, scale):
    return pl.pallas_call(
        lambda *refs: final_body(scale, *refs),
        out_shape=jax.ShapeDtypeStruct((216, 64), F32),
        in_specs=whole(2),
        out_specs=pl.BlockSpec(memory_space=pltpu.VMEM),
        compiler_params=params(),
        cost_estimate=pl.CostEstimate(flops=100_000, bytes_accessed=200_000, transcendentals=0),
        name="place_blocks",
    )(mine, theirs)


def on_device(activations, kernel, preact, upstream):
    layers = lax.axis_size("space") * activations.shape[1]
    scale = (
        1.0 / float(layers * ROWS * COLS) ** 0.5
    )
    acts, pre, ups = (array[:, 0] for array in (activations, preact, upstream))
    kern = jnp.transpose(kernel, (2, 3, 4, 0, 1)).reshape(27, CH, 64)
    other = lax.ppermute(acts, "filt", HALF)
    mine = mask_call(pre, ups, kern)
    masked = [mine] + [lax.ppermute(mine, "filt", pairs) for pairs in Y_OTHERS]
    m1, m2, m3, _ = lax.optimization_barrier((*masked[1:], other))
    masked = [mine, m1, m2, m3]
    to_inner, mid, to_outer = data_call(masked)
    both = jnp.concatenate([acts, other], axis=0)
    inner, outer = lax.ppermute(both, "space", CORE), lax.ppermute(both, "space", OUTER)
    keep, send = weight_call(masked, (acts, other, inner, outer))

    terms = keep + lax.ppermute(send, "space", CORE)
    terms = sum([lax.ppermute(terms, "space", pairs) for pairs in X_OTHERS], terms)
    layer = mid + lax.ppermute(to_inner, "space", CORE) + lax.ppermute(to_outer, "space", OUTER)
    terms, layer = lax.optimization_barrier((terms, layer))
    terms = sum([lax.ppermute(terms, "space", pairs) for pairs in Z_OTHERS], terms)
    blocks = [terms[24 * j : 24 * j + 24] for j in range(4)]
    got = [lax.ppermute(block, "filt", pairs) for block, pairs in zip(blocks[1:], Y_BACK)]
    mine_blocks = jnp.concatenate([blocks[0]] + got, axis=0)
    their_blocks = lax.ppermute(mine_blocks, "space", CORE)
    grads = final_call(mine_blocks, their_blocks, scale)
    kernel_grad = jnp.transpose(grads.reshape(3, 3, 3, CH, 64), (3, 4, 0, 1, 2))

    own, away = layer[: CH * ROWS], layer[CH * ROWS :]
    own = own + lax.ppermute(away, "filt", HALF)
    input_grad = own.astype(BF).reshape(CH, 1, ROWS, COLS)
    return (input_grad, kernel_grad)


def solution(mesh):
    in_specs = (
        P("filt", "space", None, None),
        P("filt", None, None, None, None),
        P("filt", "space", None, None),
        P("filt", "space", None, None),
    )
    out_specs = (P("filt", "space", None, None), P("filt", None, None, None, None))
    return jax.shard_map(
        on_device, mesh=mesh, in_specs=in_specs, out_specs=out_specs, check_vma=False
    )
```

```python
import jax
import jax.numpy as jnp
from jax import lax
from jax.experimental import pallas as pl
from jax.experimental.pallas import tpu as pltpu
from jax.sharding import PartitionSpec as P

ROWS, COLS, CH = 56, 128, 8
BF, F32 = jnp.bfloat16, jnp.float32
COST = 20_000_000_000


def space_pairs(to):
    pairs = []
    for i in range(32):
        z, x, core = to(i >> 3, (i >> 1) & 3, i & 1)
        pairs.append((i, ((z % 4) * 4 + x % 4) * 2 + core))
    return pairs


def filt_pairs(to):
    pairs = []
    for i in range(8):
        h, y = to(i >> 2, i & 3)
        pairs.append((i, h * 4 + y % 4))
    return pairs


OUTER = [pair for i in range(1, 31, 2) for pair in ((i, i + 1), (i + 1, i))]
CORE = space_pairs(lambda z, x, core: (z, x, core ^ 1))
X_OTHERS = [space_pairs(lambda z, x, core, j=j: (z, x + j, core)) for j in (1, 3, 2)]
Z_OTHERS = [space_pairs(lambda z, x, core, j=j: (z ^ j, x, core)) for j in (1, 2, 3)]
HALF = filt_pairs(lambda h, y: (h ^ 1, y))
Y_OTHERS = [filt_pairs(lambda h, y, j=j: (h, y + j)) for j in (1, 3, 2)]
Y_BACK = [filt_pairs(lambda h, y, j=j: (h, y - j)) for j in (1, 3, 2)]


def place():
    space, filt = lax.axis_index("space"), lax.axis_index("filt")
    return space % 2, filt // 4, filt % 4


def params():
    return pltpu.CompilerParams(vmem_limit_bytes=40 * 1024 * 1024)


def whole(count):
    return [pl.BlockSpec(memory_space=pltpu.VMEM)] * count


def mask_body(pre_hbm, up_hbm, kern_hbm, out_ref, pre_ref, up_ref, kern_ref, sems):
    pairs = ((pre_hbm, pre_ref), (up_hbm, up_ref), (kern_hbm, kern_ref))
    copies = [pltpu.make_async_copy(src, dst, sems.at[i]) for i, (src, dst) in enumerate(pairs)]
    for copy in copies:
        copy.start()
    copies[0].wait()
    copies[1].wait()
    for f in range(CH):
        keep = pre_ref[f].astype(F32) > 0
        out_ref[f] = jnp.where(keep, up_ref[f].astype(F32), 0.0).astype(BF)
    copies[2].wait()
    blank = jnp.zeros((CH, 64), F32)
    for plane in range(2):
        pieces = []
        for k2 in range(7 * plane, 7 * plane + 7):
            even = kern_ref[2 * k2].astype(F32)
            odd = kern_ref[2 * k2 + 1].astype(F32) if 2 * k2 + 1 < 27 else blank
            pieces.append(jnp.concatenate([even, odd], axis=1))
        out_ref[CH + plane] = jnp.concatenate(pieces, axis=0).astype(BF)


def mask_call(preact, upstream, kern):
    return pl.pallas_call(
        mask_body,
        out_shape=jax.ShapeDtypeStruct((CH + 2, ROWS, COLS), BF),
        in_specs=[pl.BlockSpec(memory_space=pl.ANY)] * 3,
        out_specs=pl.BlockSpec(memory_space=pltpu.VMEM),
        scratch_shapes=[
            pltpu.VMEM((CH, ROWS, COLS), BF),
            pltpu.VMEM((CH, ROWS, COLS), BF),
            pltpu.VMEM((27, CH, 64), BF),
            pltpu.SemaphoreType.DMA((3,)),
        ],
        cost_estimate=pl.CostEstimate(flops=COST, bytes_accessed=500_000, transcendentals=0),
        name="mask",
    )(preact, upstream, kern)


def spread(ref, planes, scratch):
    for ch in range(planes):
        scratch[pl.ds(ch * ROWS, ROWS), :] = ref[ch].astype(F32)


def spread_either(first, ref, other, planes, scratch):
    for ch in range(planes):
        value = jnp.where(first, ref[ch].astype(F32), other[ch].astype(F32))
        scratch[pl.ds(ch * ROWS, ROWS), :] = value


def row_of(scratch, row):
    return scratch[pl.ds(row, CH, stride=ROWS), :]


def column_shifts(scratch, row, lane):
    block = row_of(scratch, row)
    left = jnp.where(lane == COLS - 1, 0.0, pltpu.roll(block, COLS - 1, 1))
    right = jnp.where(lane == 0, 0.0, pltpu.roll(block, 1, 1))
    return [left, block, right]


def shifted_rows(scratches, rows, lane):
    columns = []
    for row in rows:
        pieces = []
        for scratch in scratches:
            pieces += column_shifts(scratch, row, lane)
        columns.append(jnp.concatenate(pieces, axis=0).astype(BF))
    return jnp.concatenate(columns, axis=1)


def packed(part, lane):
    tiles = []
    for j in range(4):
        one, two, three = (part[24 * j + 8 * kx : 24 * j + 8 * kx + 8] for kx in range(3))
        two = pltpu.roll(two, 72, 1)
        tiles += [jnp.where(lane < 72, one, two), jnp.where(lane < 16, two, pltpu.roll(three, 16, 1))]
    return jnp.concatenate(tiles, axis=0)


def unpacked(left, right, lane):
    two = jnp.where(lane < 56, pltpu.roll(left, 56, 1), pltpu.roll(right, 56, 1))
    return jnp.concatenate([left, two, pltpu.roll(right, 112, 1)], axis=0)


def weight_body(m0, m1, m2, m3, *refs):
    acts, (keep_ref, send_ref), scratch = refs[:4], refs[4:6], refs[6:]
    core, _, _ = place()
    masked, planes = scratch[:4], scratch[4:]
    for ref, buf in zip((m0, m1, m2, m3), masked):
        spread(ref, CH, buf)
    first_core = core == 0
    inner, outer = acts[2:]
    for block in range(2):
        below, here, above = planes[3 * block : 3 * block + 3]
        near, far = (ref.at[pl.ds(CH * block, CH)] for ref in (inner, outer))
        spread_either(first_core, far, near, CH, below)
        spread(acts[block], CH, here)
        spread_either(first_core, near, far, CH, above)
    lane = lax.broadcasted_iota(jnp.int32, (CH, COLS), 1)
    zero = jnp.zeros((CH, COLS), F32)
    gap = jnp.zeros((COLS - 9 * CH, COLS), F32)
    total = jnp.zeros((96, 256), F32)
    step = 8
    for first in range(0, ROWS, step):
        rows = range(first, first + step)
        lhs = shifted_rows(masked, rows, lane)
        columns = []
        for row in rows:
            pieces = []
            for block in range(2):
                for kz in range(3):
                    for ky in range(3):
                        at = row + ky - 1
                        inside = 0 <= at < ROWS
                        pieces.append(row_of(planes[3 * block + kz], at) if inside else zero)
                pieces.append(gap)
            columns.append(jnp.concatenate(pieces, axis=0).astype(BF))
        rhs = jnp.concatenate(columns, axis=1)
        total = total + lax.dot_general(
            lhs, rhs, (((1,), (1,)), ((), ())), preferred_element_type=F32
        )
    own, other = packed(total[:, :COLS], lane), packed(total[:, COLS:], lane)
    keep_ref[...] = jnp.where(first_core, own, other)
    send_ref[...] = jnp.where(first_core, other, own)


def weight_call(masked, acts):
    shape = jax.ShapeDtypeStruct((64, COLS), F32)
    return pl.pallas_call(
        weight_body,
        out_shape=(shape, shape),
        in_specs=whole(8),
        out_specs=tuple(whole(2)),
        scratch_shapes=[pltpu.VMEM((CH * ROWS, COLS), F32)] * 10,
        compiler_params=params(),
        cost_estimate=pl.CostEstimate(
            flops=COST, bytes_accessed=1_500_000, transcendentals=0
        ),
        name="weight_grad",
    )(*masked, *acts)


def data_body(m0, m1, m2, m3, inner_ref, mid_ref, outer_ref, *masked):
    core, half, y = place()
    first_core = core == 0
    for ref, buf in zip((m0, m1, m2, m3), masked):
        spread(ref, CH, buf)
    lane = lax.broadcasted_iota(jnp.int32, (CH, COLS), 1)
    rows = []
    for ref in (m0, m1, m2, m3):
        parts = [ref[CH].astype(F32), ref[CH + 1].astype(F32)]
        for kx in range(3):
            sums = [jnp.zeros((CH, COLS), F32) for _ in range(2)]
            for q in range(9):
                k = 3 * q + kx
                pair, odd = k // 2, k % 2
                value = parts[pair // 7][(pair % 7) * CH : (pair % 7 + 1) * CH]
                for block in range(2):
                    start = 8 * (4 * (half ^ block) + y)
                    shift = lax.rem(8 * q + 256 - 64 * odd - start, 128)
                    moved = pltpu.roll(value, shift, 1)
                    here = (lane >= 8 * q) & (lane < 8 * q + 8)
                    sums[block] = jnp.where(here, moved, sums[block])
            rows.append(jnp.concatenate(sums, axis=1))
    weights = jnp.concatenate(rows + [jnp.zeros((32, 256), F32)], axis=0)
    weights = jnp.transpose(weights)
    weights = jnp.concatenate([weights[:72, :96], weights[128:200, :96]], axis=0).astype(BF)
    sums = {}
    step = 4
    for first in range(0, ROWS, step):
        got = jnp.dot(
            weights, shifted_rows(masked, range(first, first + step), lane), preferred_element_type=F32
        )
        for i in range(step):
            row = first + i
            for block in range(2):
                for kz in range(3):
                    for ky in range(3):
                        at = row + ky - 1
                        if not 0 <= at < ROWS:
                            continue
                        top = ((block * 3 + kz) * 3 + ky) * CH
                        term = got[top : top + CH, i * COLS : (i + 1) * COLS]
                        key = (block, kz, at)
                        sums[key] = sums[key] + term if key in sums else term
                done = [row - 1] if row < ROWS - 1 else [row - 1, row]
                for at in done:
                    if at >= 0:
                        down, mid, up = (sums.pop((block, kz, at)) for kz in range(3))
                        place_at = pl.ds(block * CH * ROWS + at, CH, stride=ROWS)
                        mid_ref[place_at, :] = mid
                        inner_ref[place_at, :] = jnp.where(first_core, up, down)
                        outer_ref[place_at, :] = jnp.where(first_core, down, up)


def data_call(masked):
    shape = jax.ShapeDtypeStruct((2 * CH * ROWS, COLS), F32)
    return pl.pallas_call(
        data_body,
        out_shape=(shape, shape, shape),
        in_specs=whole(4),
        out_specs=tuple(whole(3)),
        scratch_shapes=[pltpu.VMEM((CH * ROWS, COLS), F32)] * 4,
        compiler_params=params(),
        cost_estimate=pl.CostEstimate(
            flops=COST, bytes_accessed=2_000_000, transcendentals=0
        ),
        name="data_grad",
    )(*masked)


def final_body(scale, mine_ref, theirs_ref, out_ref):
    core, half, y = place()
    lane = lax.broadcasted_iota(jnp.int32, (24, COLS), 1)
    sources = []
    for ref, part in ((mine_ref, half ^ core), (theirs_ref, half ^ core ^ 1)):
        for j, away in enumerate((0, 1, 3, 2)):
            block = 4 * part + lax.rem(y + away, 4)
            left, right = ref[16 * j : 16 * j + 8], ref[16 * j + 8 : 16 * j + 16]
            sources.append((block, unpacked(left, right, lane[:8])))
    for q in range(9):
        total = jnp.zeros((24, COLS), F32)
        for block, value in sources:
            moved = pltpu.roll(value, lax.rem(8 * block + 128 - 8 * q, 128), 1)
            here = (lane >= 8 * block) & (lane < 8 * block + 8)
            total = jnp.where(here, moved, total)
        out_ref[24 * q : 24 * q + 24] = (total * scale)[:, :64]


def final_call(mine, theirs, scale):
    return pl.pallas_call(
        lambda *refs: final_body(scale, *refs),
        out_shape=jax.ShapeDtypeStruct((216, 64), F32),
        in_specs=whole(2),
        out_specs=pl.BlockSpec(memory_space=pltpu.VMEM),
        compiler_params=params(),
        cost_estimate=pl.CostEstimate(flops=100_000, bytes_accessed=200_000, transcendentals=0),
        name="place_blocks",
    )(mine, theirs)


def on_device(activations, kernel, preact, upstream):
    layers = lax.axis_size("space") * activations.shape[1]
    scale = (
        1.0 / float(layers * ROWS * COLS) ** 0.5
    )
    acts, pre, ups = (array[:, 0] for array in (activations, preact, upstream))
    kern = jnp.transpose(kernel, (2, 3, 4, 0, 1)).reshape(27, CH, 64)
    other = lax.ppermute(acts, "filt", HALF)
    mine = mask_call(pre, ups, kern)
    masked = [mine] + [lax.ppermute(mine, "filt", pairs) for pairs in Y_OTHERS]
    m1, m2, m3, _ = lax.optimization_barrier((*masked[1:], other))
    masked = [mine, m1, m2, m3]
    to_inner, mid, to_outer = data_call(masked)
    both = jnp.concatenate([acts, other], axis=0)
    inner, outer = lax.ppermute(both, "space", CORE), lax.ppermute(both, "space", OUTER)
    keep, send = weight_call(masked, (acts, other, inner, outer))

    terms = keep + lax.ppermute(send, "space", CORE)
    terms = sum([lax.ppermute(terms, "space", pairs) for pairs in X_OTHERS], terms)
    layer = mid + lax.ppermute(to_inner, "space", CORE) + lax.ppermute(to_outer, "space", OUTER)
    terms, layer = lax.optimization_barrier((terms, layer))
    terms = sum([lax.ppermute(terms, "space", pairs) for pairs in Z_OTHERS], terms)
    blocks = [terms[16 * j : 16 * j + 16] for j in range(4)]
    got = [lax.ppermute(block, "filt", pairs) for block, pairs in zip(blocks[1:], Y_BACK)]
    mine_blocks = jnp.concatenate([blocks[0]] + got, axis=0)
    their_blocks = lax.ppermute(mine_blocks, "space", CORE)
    grads = final_call(mine_blocks, their_blocks, scale)
    kernel_grad = jnp.transpose(grads.reshape(3, 3, 3, CH, 64), (3, 4, 0, 1, 2))

    own, away = layer[: CH * ROWS], layer[CH * ROWS :]
    own = own + lax.ppermute(away, "filt", HALF)
    input_grad = own.astype(BF).reshape(CH, 1, ROWS, COLS)
    return (input_grad, kernel_grad)


def solution(mesh):
    in_specs = (
        P("filt", "space", None, None),
        P("filt", None, None, None, None),
        P("filt", "space", None, None),
        P("filt", "space", None, None),
    )
    out_specs = (P("filt", "space", None, None), P("filt", None, None, None, None))
    return jax.shard_map(
        on_device, mesh=mesh, in_specs=in_specs, out_specs=out_specs, check_vma=False
    )
```
